32 devices in a mesh: group: 2 (over y), dp: 16 (over z, x, core).
Axes of the slice: x: 2, y: 2, z: 4, core: 2. Of those that a mesh axis runs over, the one named last changes fastest.
Arguments:
- tokens: bfloat16 [4096, 8192], P(('group', 'dp')), parts along dimension 0, may hold values from -6 to 6
- output_cotangent: bfloat16 [4096, 512], P(('group', 'dp')), parts along dimension 0, may hold values from -6 to 6
- frozen_value_weight: bfloat16 [8192, 512], P('dp'), may hold values from -0.0625 to 0.0625
- adapter_lowering: bfloat16 [256, 16, 8192], P(('group', 'dp')), parts along dimension 0, may hold values from -0.0625 to 0.0625
- adapter_raising: bfloat16 [256, 16, 512], P(('group', 'dp')), parts along dimension 0, may hold values from -0.25 to 0.25
- tenant: int32 [4096], P(('group', 'dp')), parts along dimension 0, may hold values from 0 to 127, as said below
- tenant_row_index: int32 [256], P('group'), parts along dimension 0, may hold values from 0 to 127, as said below
Outputs:
- projected: bfloat16 [4096, 512], P(('group', 'dp')), parts along dimension 0
- token_input_grad: bfloat16 [4096, 8192], P(('group', 'dp')), parts along dimension 0
- grad_down: bfloat16 [256, 16, 8192], P(('group', 'dp')), parts along dimension 0
- grad_up: bfloat16 [256, 16, 512], P(('group', 'dp')), parts along dimension 0
The draws below stay inside these ranges and needn't reach their ends.
There are 2 independent parts, one for each index of `group`. The reference program is written for one: setup_inputs(seed, part) draws one part's arguments, and reference() takes and returns one part's arrays. A program takes and returns all parts, laid end to end along the dimension named above; an argument that names none is the same for every part. Nothing has to cross between parts.
Inputs may be any that keep to these rules, and one draw needn't show every extreme that they name: tenant[i] is the adapter of token i. The 128 tokens of device k form 4 runs of consecutive tokens, each run of one adapter; every run's adapter has its row (tenant_row_index of it) among the rows of device k - 1, k or k + 1, taken modulo 16, where device j holds rows 8 * j to 8 * j + 7. In every draw each device has runs on the rows of all three of these devices. A permutation: adapter a is row tenant_row_index[a] of adapter_lowering and adapter_raising.
All inputs are finite; a program needn't handle non-finite values.
Results may differ from the reference program's by a relative error of at most 0.0051.
Values may be sent and summed in bfloat16 or wider, within the bound.
A program may use at most 128 MiB of HBM per device.

```python
import jax
import jax.numpy as jnp
from jax import lax

MODEL_DIM = 8192
VALUE_SPAN = 512
ADAPTER_RANK = 16
ADP_DEV = 8
TOK_DEV = 128
TOKEN_COUNT = 2048
ADAPTER_COUNT = 128


def owner_rows(key):
    return jax.random.permutation(jax.random.fold_in(key, 11), ADAPTER_COUNT).astype(jnp.int32)


def draw_tenant_row_index(key, part):
    placed = owner_rows(key)
    return placed


def draw_tenant(key, part):
    placed = owner_rows(key)
    key = jax.random.fold_in(key, 5)
    devices = TOKEN_COUNT // TOK_DEV
    quarter = TOK_DEV // 4
    reach = quarter // 2 - 1

    def one_device(device_index):
        device_key = jax.random.fold_in(key, 100 + device_index)
        jitter = jax.random.randint(jax.random.fold_in(device_key, 1), (3,), -reach, reach + 1).astype(jnp.int32)
        starts = jnp.arange(1, 4, dtype=jnp.int32) * quarter + jitter
        position = jnp.arange(TOK_DEV, dtype=jnp.int32)
        run_of = jnp.sum((position[:, None] >= starts[None, :]).astype(jnp.int32), axis=1)
        last_side = jax.random.randint(jax.random.fold_in(device_key, 2), (1,), 0, 3).astype(jnp.int32)
        side = jnp.concatenate([jnp.arange(3, dtype=jnp.int32), last_side])
        owner = (device_index + side - 1 + devices) % devices
        in_store = jax.random.randint(jax.random.fold_in(device_key, 3), (4,), 0, ADP_DEV).astype(jnp.int32)
        run_rows = owner * ADP_DEV + in_store
        return jnp.take(run_rows, run_of).astype(jnp.int32)
    row_index = jax.vmap(one_device)(jnp.arange(devices, dtype=jnp.int32)).reshape(-1)
    inverse = jnp.argsort(placed).astype(jnp.int32)
    return inverse[row_index].astype(jnp.int32)


def level_of(rng, extent, pieces, smallest, high):
    def one(axis_at, parts):
        steps = jax.random.uniform(jax.random.fold_in(jax.random.fold_in(rng, 6), axis_at), (parts,), jnp.float32, smallest / len(pieces), high / len(pieces))
        return jnp.repeat(jnp.exp(steps), extent[axis_at] // parts).reshape((-1,) + (1,) * (len(extent) - axis_at - 1))

    level = one(*pieces[0])
    for cut in pieces[1:]:
        level = level * one(*cut)
    return level


def gaussian(rng, shape, deviation, most, split=(), kind=jnp.bfloat16):
    values = jax.random.normal(rng, shape, jnp.float32) * deviation
    if len(split) > 0:
        values = level_of(rng, shape, split, -0.22, 0.18) * values
    return jnp.clip(values, min=-most, max=most).astype(kind)


def setup_inputs(seed: int = 0, part: int = 0) -> dict:
    arg_keys = jax.random.split(jax.random.key(seed), 8)
    part_keys = jax.random.split(jax.random.fold_in(arg_keys[7], part), 8)
    return {
        "tokens": gaussian(part_keys[0], (TOKEN_COUNT, MODEL_DIM), 1.0, 6.0, ((0, 16),)),
        "output_cotangent": gaussian(part_keys[1], (TOKEN_COUNT, VALUE_SPAN), 1.0, 6.0, ((0, 16),)),
        "frozen_value_weight": gaussian(arg_keys[2], (MODEL_DIM, VALUE_SPAN), MODEL_DIM ** -0.5, 0.0625, ((0, 16),)),
        "adapter_lowering": gaussian(part_keys[3], (ADAPTER_COUNT, ADAPTER_RANK, MODEL_DIM), MODEL_DIM ** -0.5, 0.0625, ((0, 16),)),
        "adapter_raising": gaussian(part_keys[4], (ADAPTER_COUNT, ADAPTER_RANK, VALUE_SPAN), VALUE_SPAN ** -0.5, 0.25, ((0, 16),)),
        "tenant": draw_tenant(jax.random.fold_in(jax.random.fold_in(arg_keys[7], part), 71), part),
        "tenant_row_index": draw_tenant_row_index(jax.random.fold_in(jax.random.fold_in(arg_keys[7], part), 71), part),
    }


def reference(tokens, output_cotangent, frozen_value_weight, adapter_lowering, adapter_raising, tenant, tenant_row_index):
    row_index = jnp.take(tenant_row_index, tenant).astype(jnp.int32)
    frozen_output = jnp.dot(tokens, frozen_value_weight, preferred_element_type=jnp.float32)
    frozen_input_grad = jnp.dot(output_cotangent, frozen_value_weight.T, preferred_element_type=jnp.float32)
    blocks = TOKEN_COUNT // TOK_DEV
    token_tiles = tokens.reshape(blocks, TOK_DEV, MODEL_DIM)
    gradient_tiles = output_cotangent.reshape(blocks, TOK_DEV, VALUE_SPAN)
    tenant_index_tiles = row_index.reshape(blocks, TOK_DEV)

    def gather_totals(partial_value, batch_item):
        lowering_grad_sum, raising_grad_sum = partial_value
        token_block, grad_block, tenant_index_tile = batch_item
        lowering_block = adapter_lowering[tenant_index_tile].astype(jnp.float32)
        raising_block = adapter_raising[tenant_index_tile].astype(jnp.float32)
        token_wide = token_block.astype(jnp.float32)
        grad_wide = grad_block.astype(jnp.float32)
        narrow_rank_rows = jnp.einsum('brd,bd->br', lowering_block, token_wide).astype(jnp.bfloat16)
        reverse_rank_rows = jnp.einsum('brn,bn->br', raising_block, grad_wide).astype(jnp.bfloat16)
        adapter_output = jnp.einsum('ke,keu->ku', narrow_rank_rows.astype(jnp.float32), raising_block).astype(jnp.bfloat16)
        adapter_input_grad = jnp.einsum('yi,yiw->yw', reverse_rank_rows.astype(jnp.float32), lowering_block).astype(jnp.bfloat16)
        lowering_grad_sum = lowering_grad_sum.at[tenant_index_tile].add(reverse_rank_rows.astype(jnp.float32)[:, :, None] * token_wide[:, None, :])
        raising_grad_sum = raising_grad_sum.at[tenant_index_tile].add(narrow_rank_rows.astype(jnp.float32)[:, :, None] * grad_wide[:, None, :])
        return (lowering_grad_sum, raising_grad_sum), (adapter_output, adapter_input_grad)

    initial_totals = (jnp.zeros((ADAPTER_COUNT, ADAPTER_RANK, MODEL_DIM), jnp.float32), jnp.zeros((ADAPTER_COUNT, ADAPTER_RANK, VALUE_SPAN), jnp.float32))
    (lowering_grad_sum, raising_grad_sum), (adapter_output, adapter_input_grad) = lax.scan(gather_totals, initial_totals, (token_tiles, gradient_tiles, tenant_index_tiles))
    projected = (frozen_output + adapter_output.reshape(TOKEN_COUNT, VALUE_SPAN).astype(jnp.float32)).astype(jnp.bfloat16)
    token_input_grad = (frozen_input_grad + adapter_input_grad.reshape(TOKEN_COUNT, MODEL_DIM).astype(jnp.float32)).astype(jnp.bfloat16)
    return projected, token_input_grad, lowering_grad_sum.astype(jnp.bfloat16), raising_grad_sum.astype(jnp.bfloat16)
```

```python
import functools

import jax
import jax.numpy as jnp
from jax import lax
from jax.experimental import pallas as pl
from jax.experimental.pallas import tpu as pltpu
from jax.sharding import PartitionSpec as P

F32 = jnp.float32
BF16 = jnp.bfloat16
LAST = (((1,), (1,)), ((), ()))
FIRST = (((0,), (0,)), ((), ()))
TILE = 512


def dot(a, b, dims=None):
    if dims is None:
        return jnp.dot(a, b, preferred_element_type=F32)
    return lax.dot_general(a, b, dims, preferred_element_type=F32)


def kernel(
    planes, chips, tok, ct, w, low, rai, mask, sel,
    proj, tgrad, gdown, gup,
    full, near, packed, part, inc, req, acc,
    zs, zr, xs, xr, cs, cr, qs, qr, ps, pr, gs, gr,
):
    count = planes * chips * 2
    rows = w.shape[0]
    model = tok.shape[1]
    wide = near.shape[1]
    side = sel.shape[1]
    plane = chips * 2 * rows
    me = lax.axis_index("dp")
    core = lax.rem(me, 2)
    chip = lax.rem(me // 2, chips)
    level = me // (2 * chips)
    left, right = lax.rem(me + count - 1, count), lax.rem(me + 1, count)

    def at(z, x, c):
        return (lax.rem(z, planes) * chips + lax.rem(x, chips)) * 2 + c

    def block(owner):
        return full.at[pl.ds(pl.multiple_of(owner * rows, rows), rows)]

    def remote(src, dst, send, recv, device):
        copy = pltpu.make_async_remote_copy(
            src_ref=src, dst_ref=dst, send_sem=send, recv_sem=recv,
            device_id={"dp": device}, device_id_type=pl.DeviceIdType.MESH,
        )
        copy.start()
        return copy

    mates = [at(level, chip, 1 - core), left, right]
    mates += [at(level + dz, chip, core) for dz in range(1, planes)]
    mates += [at(level, chip + dx, core) for dx in range(1, chips)]
    barrier = pltpu.get_barrier_semaphore()
    for mate in mates:
        pl.semaphore_signal(
            barrier, inc=1, device_id={"dp": mate}, device_id_type=pl.DeviceIdType.MESH
        )
    pl.semaphore_wait(barrier, len(mates))

    sent = []
    ask = [
        remote(sel.at[0], req.at[1], qs.at[0], qr.at[0], left),
        remote(sel.at[2], req.at[0], qs.at[1], qr.at[1], right),
    ]
    across, beside, over = {}, {}, {}

    def spread_core(dz, dx):
        owner = at(level + planes - dz, chip + chips - dx, core)
        src = w if dz == 0 and dx == 0 else block(owner)
        n = dz * chips + dx
        over[dz, dx] = remote(src, block(owner), cs.at[n], cr.at[n], at(level, chip, 1 - core))

    def spread_chip(dz):
        owner = at(level + planes - dz, chip, core)
        src = w if dz == 0 else block(owner)
        for dx in range(1, chips):
            n = dz * (chips - 1) + dx - 1
            beside[dz, dx] = remote(
                src, block(owner), xs.at[n], xr.at[n], at(level, chip + dx, core)
            )

    order = sorted(range(1, planes), key=lambda d: min(d, planes - d))
    spread_chip(0)
    for dz in order:
        across[dz] = remote(
            w, block(me), zs.at[dz - 1], zr.at[dz - 1], at(level + dz, chip, core)
        )
    spread_core(0, 0)
    block(me)[...] = w[...]

    for s, (asked, device, slot) in enumerate(((1, left, 2), (0, right, 0))):
        ask[asked].wait_recv()

        @pl.loop(0, model // TILE)
        def _(i, s=s):
            cols = pl.ds(pl.multiple_of(i * TILE, TILE), TILE)
            packed[s, :, cols] = dot(req[s], low[:, cols]).astype(BF16)

        packed[s, :, pl.ds(model, wide - model)] = dot(req[s], rai[...]).astype(BF16)
        sent.append(
            remote(
                packed.at[s], near.at[pl.ds(slot * side, side)], ps.at[s], pr.at[s], device
            )
        )
    fetched = list(sent)

    @pl.loop(0, model // TILE)
    def _(i):
        cols = pl.ds(pl.multiple_of(i * TILE, TILE), TILE)
        near[pl.ds(side, side), cols] = dot(sel[1], low[:, cols]).astype(BF16)

    near[pl.ds(side, side), pl.ds(model, wide - model)] = dot(sel[1], rai[...]).astype(BF16)

    def arrive(dz):
        if dz:
            across[dz].wait_recv()
            spread_chip(dz)
            spread_core(dz, 0)

    if planes > 1:
        arrive(order[0])

    for copy in fetched:
        copy.wait_recv()

    def narrow_step(i, total):
        cols = pl.ds(pl.multiple_of(i * TILE, TILE), TILE)
        return total + dot(tok[:, cols], near[:, cols], LAST)

    narrow = lax.fori_loop(
        0, model // TILE, narrow_step, jnp.zeros((tok.shape[0], 3 * side), F32)
    )
    narrow = (narrow * mask[...]).astype(BF16)
    raising = near[:, pl.ds(model, wide - model)]
    back = (dot(ct[...], raising, LAST) * mask[...]).astype(BF16)

    @pl.loop(0, model // TILE)
    def _(i):
        cols = pl.ds(pl.multiple_of(i * TILE, TILE), TILE)
        terms = dot(back, tok[:, cols], FIRST).astype(BF16)
        part[0, :, cols] = terms[:side]
        part[1, :, cols] = terms[2 * side :]

    terms = dot(narrow, ct[...], FIRST).astype(BF16)
    part[0, :, pl.ds(model, wide - model)] = terms[:side]
    part[1, :, pl.ds(model, wide - model)] = terms[2 * side :]
    back_terms = [
        remote(part.at[0], inc.at[1], gs.at[0], gr.at[0], left),
        remote(part.at[1], inc.at[0], gs.at[1], gr.at[1], right),
    ]

    def use(dz):
        for dx in range(1, chips):
            beside[dz, dx].wait_recv()
            spread_core(dz, dx)

    def finish(dz):
        for dx in range(chips):
            over[dz, dx].wait_recv()
        start = lax.rem(level + planes - dz, planes) * plane

        @pl.loop(0, plane // TILE)
        def _(i):
            span = pl.ds(pl.multiple_of(start + i * TILE, TILE), TILE)
            held = full[span, :]
            acc[...] += dot(tok[:, span], held)
            lora = dot(back, near[:, span]).astype(BF16).astype(F32)
            tgrad[:, span] = (dot(ct[...], held, LAST) + lora).astype(BF16)

    acc[...] = jnp.zeros_like(acc)
    use(0)
    for dz in order[1:]:
        arrive(dz)
    finish(0)
    for dz in order:
        use(dz)
        if dz == order[-1]:
            for copy in back_terms:
                copy.wait_recv()
            own_back = dot(back[:, side : 2 * side], sel[1]).astype(BF16)
            own_narrow = dot(narrow[:, side : 2 * side], sel[1]).astype(BF16)

            @pl.loop(0, model // TILE)
            def _(i):
                cols = pl.ds(pl.multiple_of(i * TILE, TILE), TILE)
                gdown[:, cols] = (
                    dot(own_back, tok[:, cols], FIRST)
                    + dot(req[0], inc[0, :, cols], FIRST)
                    + dot(req[1], inc[1, :, cols], FIRST)
                ).astype(BF16)

            tail = pl.ds(model, wide - model)
            gup[...] = (
                dot(own_narrow, ct[...], FIRST)
                + dot(req[0], inc[0, :, tail], FIRST)
                + dot(req[1], inc[1, :, tail], FIRST)
            ).astype(BF16)
        finish(dz)
    proj[...] = (acc[...] + dot(narrow, raising).astype(BF16).astype(F32)).astype(BF16)

    for copy in (
        ask + sent + back_terms + list(across.values()) + list(beside.values())
        + list(over.values())
    ):
        copy.wait_send()


def body(tokens, output_cotangent, weight, lowering, raising, tenant, tenant_row_index):
    count = lax.axis_size("dp")
    here = lax.axis_index("dp")
    chips = 2 if count < 64 else 4
    planes = count // (2 * chips)
    token_count, model = tokens.shape
    value = output_cotangent.shape[1]
    stored, rank = lowering.shape[:2]
    ranks = stored * rank
    row = jnp.take(tenant_row_index, tenant)
    owner = row // stored
    side = (owner - here + 1 + count) % count
    local = row % stored
    on = side[:, None] == jnp.arange(3)[None, :]
    lo = jnp.min(jnp.where(on, local[:, None], stored - 1), axis=0)
    hi = jnp.max(jnp.where(on, local[:, None], 0), axis=0)
    slots = jnp.stack([lo, hi], axis=1)
    hit = on[:, :, None] & (local[:, None, None] == slots[None])
    first = hit[:, :, :1]
    hit = jnp.concatenate([first, hit[:, :, 1:] & ~first], axis=2)
    mask = jnp.broadcast_to(
        hit.reshape(token_count, 6, 1), (token_count, 6, rank)
    ).reshape(token_count, 6 * rank).astype(F32)
    wanted = slots[:, :, None] * rank + jnp.arange(rank)[None, None, :]
    sel = (
        wanted.reshape(3, 2 * rank, 1) == jnp.arange(ranks)[None, None, :]
    ).astype(BF16)
    wide = model + value
    dma = pltpu.SemaphoreType.DMA
    vmem = pl.BlockSpec(memory_space=pltpu.VMEM)
    proj, tgrad, gdown, gup = pl.pallas_call(
        functools.partial(kernel, planes, chips),
        out_shape=(
            jax.ShapeDtypeStruct((token_count, value), BF16),
            jax.ShapeDtypeStruct((token_count, model), BF16),
            jax.ShapeDtypeStruct((ranks, model), BF16),
            jax.ShapeDtypeStruct((ranks, value), BF16),
        ),
        in_specs=[vmem] * 7,
        out_specs=(vmem,) * 4,
        scratch_shapes=[
            pltpu.VMEM((model, value), BF16),
            pltpu.VMEM((6 * rank, wide), BF16),
            pltpu.VMEM((2, 2 * rank, wide), BF16),
            pltpu.VMEM((2, 2 * rank, wide), BF16),
            pltpu.VMEM((2, 2 * rank, wide), BF16),
            pltpu.VMEM((2, 2 * rank, ranks), BF16),
            pltpu.VMEM((token_count, value), F32),
            dma((planes,)), dma((planes,)),
            dma((planes * chips,)), dma((planes * chips,)),
            dma((planes * chips,)), dma((planes * chips,)),
            dma((2,)), dma((2,)), dma((2,)), dma((2,)), dma((2,)), dma((2,)),
        ],
        compiler_params=pltpu.CompilerParams(
            collective_id=0, has_side_effects=True, vmem_limit_bytes=48 * 1024 * 1024
        ),
        cost_estimate=pl.CostEstimate(
            flops=4 * token_count * model * value,
            bytes_accessed=8 * token_count * model,
            transcendentals=0,
        ),
    )(
        tokens, output_cotangent, weight,
        lowering.reshape(ranks, model), raising.reshape(ranks, value), mask, sel,
    )
    return (
        proj, tgrad,
        gdown.reshape(stored, rank, model), gup.reshape(stored, rank, value),
    )


def solution(mesh):
    rows = P(("group", "dp"), None)
    stacks = P(("group", "dp"), None, None)
    return jax.shard_map(
        body,
        mesh=mesh,
        in_specs=(rows, rows, P("dp", None), stacks, stacks, P(("group", "dp")), P("group")),
        out_specs=(rows, rows, stacks, stacks),
        check_vma=False,
    )
```

```python
import functools

import jax
import jax.numpy as jnp
from jax import lax
from jax.experimental import pallas as pl
from jax.experimental.pallas import tpu as pltpu
from jax.sharding import PartitionSpec as P

F32 = jnp.float32
BF16 = jnp.bfloat16
LAST = (((1,), (1,)), ((), ()))
FIRST = (((0,), (0,)), ((), ()))
TILE = 512


def dot(a, b, dims=None):
    if dims is None:
        return jnp.dot(a, b, preferred_element_type=F32)
    return lax.dot_general(a, b, dims, preferred_element_type=F32)


def kernel(
    planes, chips, tok, ct, w, low, rai, mask, sel,
    proj, tgrad, gdown, gup,
    full, near, packed, part, inc, req, acc,
    zs, zr, xs, xr, ys, yr, cs, cr, qs, qr, ps, pr, gs, gr,
):
    count = planes * chips * 2
    rows = w.shape[0]
    model = tok.shape[1]
    wide = near.shape[1]
    side = sel.shape[1]
    plane = chips * 2 * rows
    me = lax.axis_index("dp")
    core = lax.rem(me, 2)
    chip = lax.rem(me // 2, chips)
    level = me // (2 * chips)
    left, right = lax.rem(me + count - 1, count), lax.rem(me + 1, count)

    half = rows // 2
    group = lax.axis_index("group")
    mine, other = group, 1 - group

    def at(z, x, c):
        return (lax.rem(z, planes) * chips + lax.rem(x, chips)) * 2 + c

    def block(owner):
        return full.at[pl.ds(pl.multiple_of(owner * rows, rows), rows)]

    def piece(owner, part_of):
        return full.at[pl.ds(pl.multiple_of(owner * rows + part_of * half, half), half)]

    def remote(src, dst, send, recv, device, to_group=None):
        copy = pltpu.make_async_remote_copy(
            src_ref=src, dst_ref=dst, send_sem=send, recv_sem=recv,
            device_id={"group": group if to_group is None else to_group, "dp": device},
            device_id_type=pl.DeviceIdType.MESH,
        )
        copy.start()
        return copy

    mates = [(group, at(level, chip, 1 - core)), (group, left), (group, right), (other, me)]
    mates += [(group, at(level + dz, chip, core)) for dz in range(1, planes)]
    mates += [(group, at(level, chip + dx, core)) for dx in range(1, chips)]
    barrier = pltpu.get_barrier_semaphore()
    for to_group, mate in mates:
        pl.semaphore_signal(
            barrier, inc=1, device_id={"group": to_group, "dp": mate},
            device_id_type=pl.DeviceIdType.MESH,
        )
    pl.semaphore_wait(barrier, len(mates))

    sent = []
    ask = [
        remote(sel.at[0], req.at[1], qs.at[0], qr.at[0], left),
        remote(sel.at[2], req.at[0], qs.at[1], qr.at[1], right),
    ]
    across, beside, facing, over = {}, {}, {}, {}
    order = sorted(range(1, planes), key=lambda d: min(d, planes - d))
    last = order[-1]

    def source(dz, dx):
        return at(level + planes - dz, chip + chips - dx, core)

    def to_core(dz, dx, which):
        if dz == 0:
            dst = block(source(0, dx))
            src, n = (dst if dx else w), dx
        else:
            src = dst = piece(source(dz, dx), other if which else mine)
            n = chips + ((dz - 1) * chips + dx) * 2 + which
        over[dz, dx, which] = remote(
            src, dst, cs.at[n], cr.at[n], at(level, chip, 1 - core)
        )

    def to_chip(key, src, dst, first):
        for dx in range(1, chips):
            n = first * (chips - 1) + dx - 1
            beside[key, dx] = remote(src, dst, xs.at[n], xr.at[n], at(level, chip + dx, core))

    def to_group(dz, dx):
        ref = piece(source(dz, dx), mine)
        n = (dz - 1) * chips + dx
        facing[dz, dx] = remote(ref, ref, ys.at[n], yr.at[n], me, other)

    for dz in order:
        across[dz] = remote(
            w.at[pl.ds(pl.multiple_of(mine * half, half), half)], piece(me, mine),
            zs.at[dz - 1], zr.at[dz - 1], at(level + dz, chip, core),
        )
    to_chip("own", w, block(me), 0)
    to_core(0, 0, 0)
    block(me)[...] = w[...]

    for s, (asked, device, slot) in enumerate(((1, left, 2), (0, right, 0))):
        ask[asked].wait_recv()

        @pl.loop(0, model // TILE)
        def _(i, s=s):
            cols = pl.ds(pl.multiple_of(i * TILE, TILE), TILE)
            packed[s, :, cols] = dot(req[s], low[:, cols]).astype(BF16)

        packed[s, :, pl.ds(model, wide - model)] = dot(req[s], rai[...]).astype(BF16)
        sent.append(
            remote(
                packed.at[s], near.at[pl.ds(slot * side, side)], ps.at[s], pr.at[s], device
            )
        )
    fetched = list(sent)

    @pl.loop(0, model // TILE)
    def _(i):
        cols = pl.ds(pl.multiple_of(i * TILE, TILE), TILE)
        near[pl.ds(side, side), cols] = dot(sel[1], low[:, cols]).astype(BF16)

    near[pl.ds(side, side), pl.ds(model, wide - model)] = dot(sel[1], rai[...]).astype(BF16)

    def from_level(dz):
        across[dz].wait_recv()
        ref = piece(source(dz, 0), mine)
        to_group(dz, 0)
        to_chip(dz, ref, ref, dz)
        to_core(dz, 0, 0)

    def own_chip():
        for dx in range(1, chips):
            beside["own", dx].wait_recv()
            to_core(0, dx, 0)

    def from_chip(dz):
        for dx in range(1, chips):
            beside[dz, dx].wait_recv()
            if dz != last:
                to_group(dz, dx)
            to_core(dz, dx, 0)

    def from_group(dz):
        facing[dz, 0].wait_recv()
        if dz == last:
            ref = piece(source(dz, 0), other)
            to_chip("last", ref, ref, planes)
        to_core(dz, 0, 1)

    def from_corner(dz):
        for dx in range(1, chips):
            (beside["last", dx] if dz == last else facing[dz, dx]).wait_recv()
            to_core(dz, dx, 1)

    from_level(order[0])
    own_chip()
    for dz in order[1:-1]:
        from_level(dz)

    for copy in fetched:
        copy.wait_recv()

    def narrow_step(i, total):
        cols = pl.ds(pl.multiple_of(i * TILE, TILE), TILE)
        return total + dot(tok[:, cols], near[:, cols], LAST)

    narrow = lax.fori_loop(
        0, model // TILE, narrow_step, jnp.zeros((tok.shape[0], 3 * side), F32)
    )
    narrow = (narrow * mask[...]).astype(BF16)
    raising = near[:, pl.ds(model, wide - model)]
    back = (dot(ct[...], raising, LAST) * mask[...]).astype(BF16)

    @pl.loop(0, model // TILE)
    def _(i):
        cols = pl.ds(pl.multiple_of(i * TILE, TILE), TILE)
        terms = dot(back, tok[:, cols], FIRST).astype(BF16)
        part[0, :, cols] = terms[:side]
        part[1, :, cols] = terms[2 * side :]

    terms = dot(narrow, ct[...], FIRST).astype(BF16)
    part[0, :, pl.ds(model, wide - model)] = terms[:side]
    part[1, :, pl.ds(model, wide - model)] = terms[2 * side :]
    back_terms = [
        remote(part.at[0], inc.at[1], gs.at[0], gr.at[0], left),
        remote(part.at[1], inc.at[0], gs.at[1], gr.at[1], right),
    ]

    def finish(dz):
        for dx in range(chips):
            for which in range(2 if dz else 1):
                over[dz, dx, which].wait_recv()
        start = lax.rem(level + planes - dz, planes) * plane

        @pl.loop(0, plane // TILE)
        def _(i):
            span = pl.ds(pl.multiple_of(start + i * TILE, TILE), TILE)
            held = full[span, :]
            acc[...] += dot(tok[:, span], held)
            lora = dot(back, near[:, span]).astype(BF16).astype(F32)
            tgrad[:, span] = (dot(ct[...], held, LAST) + lora).astype(BF16)

    acc[...] = jnp.zeros_like(acc)
    from_chip(order[0])
    from_group(order[0])
    finish(0)
    if last != order[0]:
        from_level(last)
    for dz in order[1:-1]:
        from_chip(dz)
        from_group(dz)
    if last != order[0]:
        from_chip(last)
        from_group(last)
    for dz in order:
        from_corner(dz)
        if dz == last:
            for copy in back_terms:
                copy.wait_recv()
            own_back = dot(back[:, side : 2 * side], sel[1]).astype(BF16)
            own_narrow = dot(narrow[:, side : 2 * side], sel[1]).astype(BF16)

            @pl.loop(0, model // TILE)
            def _(i):
                cols = pl.ds(pl.multiple_of(i * TILE, TILE), TILE)
                gdown[:, cols] = (
                    dot(own_back, tok[:, cols], FIRST)
                    + dot(req[0], inc[0, :, cols], FIRST)
                    + dot(req[1], inc[1, :, cols], FIRST)
                ).astype(BF16)

            tail = pl.ds(model, wide - model)
            gup[...] = (
                dot(own_narrow, ct[...], FIRST)
                + dot(req[0], inc[0, :, tail], FIRST)
                + dot(req[1], inc[1, :, tail], FIRST)
            ).astype(BF16)
        finish(dz)
    proj[...] = (acc[...] + dot(narrow, raising).astype(BF16).astype(F32)).astype(BF16)

    for copy in (
        ask + sent + back_terms + list(across.values()) + list(beside.values())
        + list(facing.values()) + list(over.values())
    ):
        copy.wait_send()


def body(tokens, output_cotangent, weight, lowering, raising, tenant, tenant_row_index):
    count = lax.axis_size("dp")
    here = lax.axis_index("dp")
    chips = 2 if count < 64 else 4
    planes = count // (2 * chips)
    token_count, model = tokens.shape
    value = output_cotangent.shape[1]
    stored, rank = lowering.shape[:2]
    ranks = stored * rank
    row = jnp.take(tenant_row_index, tenant)
    owner = row // stored
    side = (owner - here + 1 + count) % count
    local = row % stored
    on = side[:, None] == jnp.arange(3)[None, :]
    lo = jnp.min(jnp.where(on, local[:, None], stored - 1), axis=0)
    hi = jnp.max(jnp.where(on, local[:, None], 0), axis=0)
    slots = jnp.stack([lo, hi], axis=1)
    hit = on[:, :, None] & (local[:, None, None] == slots[None])
    first = hit[:, :, :1]
    hit = jnp.concatenate([first, hit[:, :, 1:] & ~first], axis=2)
    mask = jnp.broadcast_to(
        hit.reshape(token_count, 6, 1), (token_count, 6, rank)
    ).reshape(token_count, 6 * rank).astype(F32)
    wanted = slots[:, :, None] * rank + jnp.arange(rank)[None, None, :]
    sel = (
        wanted.reshape(3, 2 * rank, 1) == jnp.arange(ranks)[None, None, :]
    ).astype(BF16)
    wide = model + value
    dma = pltpu.SemaphoreType.DMA
    vmem = pl.BlockSpec(memory_space=pltpu.VMEM)
    proj, tgrad, gdown, gup = pl.pallas_call(
        functools.partial(kernel, planes, chips),
        out_shape=(
            jax.ShapeDtypeStruct((token_count, value), BF16),
            jax.ShapeDtypeStruct((token_count, model), BF16),
            jax.ShapeDtypeStruct((ranks, model), BF16),
            jax.ShapeDtypeStruct((ranks, value), BF16),
        ),
        in_specs=[vmem] * 7,
        out_specs=(vmem,) * 4,
        scratch_shapes=[
            pltpu.VMEM((model, value), BF16),
            pltpu.VMEM((6 * rank, wide), BF16),
            pltpu.VMEM((2, 2 * rank, wide), BF16),
            pltpu.VMEM((2, 2 * rank, wide), BF16),
            pltpu.VMEM((2, 2 * rank, wide), BF16),
            pltpu.VMEM((2, 2 * rank, ranks), BF16),
            pltpu.VMEM((token_count, value), F32),
            dma((planes,)), dma((planes,)),
            dma(((planes + 1) * chips,)), dma(((planes + 1) * chips,)),
            dma((planes * chips,)), dma((planes * chips,)),
            dma((2 * planes * chips,)), dma((2 * planes * chips,)),
            dma((2,)), dma((2,)), dma((2,)), dma((2,)), dma((2,)), dma((2,)),
        ],
        compiler_params=pltpu.CompilerParams(
            collective_id=0, has_side_effects=True, vmem_limit_bytes=48 * 1024 * 1024
        ),
        cost_estimate=pl.CostEstimate(
            flops=4 * token_count * model * value,
            bytes_accessed=8 * token_count * model,
            transcendentals=0,
        ),
    )(
        tokens, output_cotangent, weight,
        lowering.reshape(ranks, model), raising.reshape(ranks, value), mask, sel,
    )
    return (
        proj, tgrad,
        gdown.reshape(stored, rank, model), gup.reshape(stored, rank, value),
    )


def solution(mesh):
    rows = P(("group", "dp"), None)
    stacks = P(("group", "dp"), None, None)
    return jax.shard_map(
        body,
        mesh=mesh,
        in_specs=(rows, rows, P("dp", None), stacks, stacks, P(("group", "dp")), P("group")),
        out_specs=(rows, rows, stacks, stacks),
        check_vma=False,
    )
```

```python
import functools

import jax
import jax.numpy as jnp
from jax import lax
from jax.experimental import pallas as pl
from jax.experimental.pallas import tpu as pltpu
from jax.sharding import PartitionSpec as P

F32 = jnp.float32
BF16 = jnp.bfloat16
LAST = (((1,), (1,)), ((), ()))
FIRST = (((0,), (0,)), ((), ()))
TILE = 2048


def dot(a, b, dims=None):
    if dims is None:
        return jnp.dot(a, b, preferred_element_type=F32)
    return lax.dot_general(a, b, dims, preferred_element_type=F32)


def kernel(
    planes, chips, tok, ct, w, low, rai, mask, sel,
    proj, tgrad, gdown, gup,
    full, near, packed, part, inc, req, acc,
    zs, zr, xs, xr, ys, yr, cs, cr, qs, qr, ps, pr, gs, gr,
):
    count = planes * chips * 2
    rows = w.shape[0]
    model = tok.shape[1]
    wide = near.shape[1]
    side = sel.shape[1]
    plane = chips * 2 * rows
    me = lax.axis_index("dp")
    core = lax.rem(me, 2)
    chip = lax.rem(me // 2, chips)
    level = me // (2 * chips)
    left, right = lax.rem(me + count - 1, count), lax.rem(me + 1, count)

    half = rows // 2
    group = lax.axis_index("group")
    mine, other = group, 1 - group

    def at(z, x, c):
        return (lax.rem(z, planes) * chips + lax.rem(x, chips)) * 2 + c

    def block(owner):
        return full.at[pl.ds(pl.multiple_of(owner * rows, rows), rows)]

    def piece(owner, part_of):
        return full.at[pl.ds(pl.multiple_of(owner * rows + part_of * half, half), half)]

    def remote(src, dst, send, recv, device, to_group=None):
        copy = pltpu.make_async_remote_copy(
            src_ref=src, dst_ref=dst, send_sem=send, recv_sem=recv,
            device_id={"group": group if to_group is None else to_group, "dp": device},
            device_id_type=pl.DeviceIdType.MESH,
        )
        copy.start()
        return copy

    mates = [(group, at(level, chip, 1 - core)), (group, left), (group, right), (other, me)]
    mates += [(group, at(level + dz, chip, core)) for dz in range(1, planes)]
    mates += [(group, at(level, chip + dx, core)) for dx in range(1, chips)]
    barrier = pltpu.get_barrier_semaphore()
    for to_group, mate in mates:
        pl.semaphore_signal(
            barrier, inc=1, device_id={"group": to_group, "dp": mate},
            device_id_type=pl.DeviceIdType.MESH,
        )
    pl.semaphore_wait(barrier, len(mates))

    sent = []
    ask = [
        remote(sel.at[0], req.at[1], qs.at[0], qr.at[0], left),
        remote(sel.at[2], req.at[0], qs.at[1], qr.at[1], right),
    ]
    across, beside, facing, over = {}, {}, {}, {}
    order = sorted(range(1, planes), key=lambda d: min(d, planes - d))
    last = order[-1]

    def source(dz, dx):
        return at(level + planes - dz, chip + chips - dx, core)

    def to_core(dz, dx, which):
        if dz == 0 and dx == 0:
            src, dst = w, block(me)
        else:
            src = dst = piece(source(dz, dx), other if which else mine)
        n = (dz * chips + dx) * 2 + which
        over[dz, dx, which] = remote(
            src, dst, cs.at[n], cr.at[n], at(level, chip, 1 - core)
        )

    def to_chip(key, src, dst, first):
        for dx in range(1, chips):
            n = first * (chips - 1) + dx - 1
            beside[key, dx] = remote(src, dst, xs.at[n], xr.at[n], at(level, chip + dx, core))

    def to_group(dz, dx):
        ref = piece(source(dz, dx), mine)
        n = dz * chips + dx
        facing[dz, dx] = remote(ref, ref, ys.at[n], yr.at[n], me, other)

    for dz in order:
        across[dz] = remote(
            w.at[pl.ds(pl.multiple_of(mine * half, half), half)], piece(me, mine),
            zs.at[dz - 1], zr.at[dz - 1], at(level + dz, chip, core),
        )
    to_chip(0, w.at[pl.ds(pl.multiple_of(mine * half, half), half)], piece(me, mine), 0)
    to_core(0, 0, 0)
    block(me)[...] = w[...]

    for s, (asked, device, slot) in enumerate(((1, left, 2), (0, right, 0))):
        ask[asked].wait_recv()

        @pl.loop(0, model // TILE)
        def _(i, s=s):
            cols = pl.ds(pl.multiple_of(i * TILE, TILE), TILE)
            packed[s, :, cols] = dot(req[s], low[:, cols]).astype(BF16)

        packed[s, :, pl.ds(model, wide - model)] = dot(req[s], rai[...]).astype(BF16)
        sent.append(
            remote(
                packed.at[s], near.at[pl.ds(slot * side, side)], ps.at[s], pr.at[s], device
            )
        )
    fetched = list(sent)

    @pl.loop(0, model // TILE)
    def _(i):
        cols = pl.ds(pl.multiple_of(i * TILE, TILE), TILE)
        near[pl.ds(side, side), cols] = dot(sel[1], low[:, cols]).astype(BF16)

    near[pl.ds(side, side), pl.ds(model, wide - model)] = dot(sel[1], rai[...]).astype(BF16)

    def from_level(dz):
        across[dz].wait_recv()
        ref = piece(source(dz, 0), mine)
        to_group(dz, 0)
        to_chip(dz, ref, ref, dz)
        to_core(dz, 0, 0)

    def from_chip(dz):
        for dx in range(1, chips):
            beside[dz, dx].wait_recv()
            to_group(dz, dx)
            to_core(dz, dx, 0)

    def from_group(dz):
        facing[dz, 0].wait_recv()
        to_core(dz, 0, 1)

    def from_corner(dz):
        for dx in range(1, chips):
            facing[dz, dx].wait_recv()
            to_core(dz, dx, 1)

    from_chip(0)
    from_level(order[0])
    for dz in order[1:-1]:
        from_level(dz)

    for copy in fetched:
        copy.wait_recv()

    def narrow_step(i, total):
        cols = pl.ds(pl.multiple_of(i * TILE, TILE), TILE)
        return total + dot(tok[:, cols], near[:, cols], LAST)

    narrow = lax.fori_loop(
        0, model // TILE, narrow_step, jnp.zeros((tok.shape[0], 3 * side), F32)
    )
    narrow = (narrow * mask[...]).astype(BF16)
    raising = near[:, pl.ds(model, wide - model)]
    back = (dot(ct[...], raising, LAST) * mask[...]).astype(BF16)

    @pl.loop(0, model // TILE)
    def _(i):
        cols = pl.ds(pl.multiple_of(i * TILE, TILE), TILE)
        terms = dot(back, tok[:, cols], FIRST).astype(BF16)
        part[0, :, cols] = terms[:side]
        part[1, :, cols] = terms[2 * side :]

    terms = dot(narrow, ct[...], FIRST).astype(BF16)
    part[0, :, pl.ds(model, wide - model)] = terms[:side]
    part[1, :, pl.ds(model, wide - model)] = terms[2 * side :]
    back_terms = [
        remote(part.at[0], inc.at[1], gs.at[0], gr.at[0], left),
        remote(part.at[1], inc.at[0], gs.at[1], gr.at[1], right),
    ]

    def finish(dz):
        for dx in range(chips):
            for which in range(2 if dz or dx else 1):
                over[dz, dx, which].wait_recv()
        start = lax.rem(level + planes - dz, planes) * plane
        step = min(plane, TILE)

        @pl.loop(0, plane // step)
        def _(i):
            span = pl.ds(pl.multiple_of(start + i * step, step), step)
            held = full[span, :]
            acc[...] += dot(tok[:, span], held)
            lora = dot(back, near[:, span]).astype(BF16).astype(F32)
            tgrad[:, span] = (dot(ct[...], held, LAST) + lora).astype(BF16)

    acc[...] = jnp.zeros_like(acc)
    from_chip(order[0])
    from_group(order[0])
    from_corner(0)
    if last != order[0]:
        from_level(last)
    finish(0)
    for dz in order[1:-1]:
        from_chip(dz)
        from_group(dz)
    from_corner(order[0])
    if last != order[0]:
        from_chip(last)
        from_group(last)
    for dz in order:
        if dz != order[0]:
            from_corner(dz)
        if dz == last:
            for copy in back_terms:
                copy.wait_recv()
            own_back = dot(back[:, side : 2 * side], sel[1]).astype(BF16)
            own_narrow = dot(narrow[:, side : 2 * side], sel[1]).astype(BF16)

            @pl.loop(0, model // TILE)
            def _(i):
                cols = pl.ds(pl.multiple_of(i * TILE, TILE), TILE)
                gdown[:, cols] = (
                    dot(own_back, tok[:, cols], FIRST)
                    + dot(req[0], inc[0, :, cols], FIRST)
                    + dot(req[1], inc[1, :, cols], FIRST)
                ).astype(BF16)

            tail = pl.ds(model, wide - model)
            gup[...] = (
                dot(own_narrow, ct[...], FIRST)
                + dot(req[0], inc[0, :, tail], FIRST)
                + dot(req[1], inc[1, :, tail], FIRST)
            ).astype(BF16)
        finish(dz)
    proj[...] = (acc[...] + dot(narrow, raising).astype(BF16).astype(F32)).astype(BF16)

    for copy in (
        ask + sent + back_terms + list(across.values()) + list(beside.values())
        + list(facing.values()) + list(over.values())
    ):
        copy.wait_send()


def body(tokens, output_cotangent, weight, lowering, raising, tenant, tenant_row_index):
    count = lax.axis_size("dp")
    here = lax.axis_index("dp")
    chips = 2 if count < 64 else 4
    planes = count // (2 * chips)
    token_count, model = tokens.shape
    value = output_cotangent.shape[1]
    stored, rank = lowering.shape[:2]
    ranks = stored * rank
    row = jnp.take(tenant_row_index, tenant)
    owner = row // stored
    side = (owner - here + 1 + count) % count
    local = row % stored
    on = side[:, None] == jnp.arange(3)[None, :]
    lo = jnp.min(jnp.where(on, local[:, None], stored - 1), axis=0)
    hi = jnp.max(jnp.where(on, local[:, None], 0), axis=0)
    slots = jnp.stack([lo, hi], axis=1)
    hit = on[:, :, None] & (local[:, None, None] == slots[None])
    first = hit[:, :, :1]
    hit = jnp.concatenate([first, hit[:, :, 1:] & ~first], axis=2)
    mask = jnp.broadcast_to(
        hit.reshape(token_count, 6, 1), (token_count, 6, rank)
    ).reshape(token_count, 6 * rank).astype(F32)
    wanted = slots[:, :, None] * rank + jnp.arange(rank)[None, None, :]
    sel = (
        wanted.reshape(3, 2 * rank, 1) == jnp.arange(ranks)[None, None, :]
    ).astype(BF16)
    wide = model + value
    dma = pltpu.SemaphoreType.DMA
    vmem = pl.BlockSpec(memory_space=pltpu.VMEM)
    proj, tgrad, gdown, gup = pl.pallas_call(
        functools.partial(kernel, planes, chips),
        out_shape=(
            jax.ShapeDtypeStruct((token_count, value), BF16),
            jax.ShapeDtypeStruct((token_count, model), BF16),
            jax.ShapeDtypeStruct((ranks, model), BF16),
            jax.ShapeDtypeStruct((ranks, value), BF16),
        ),
        in_specs=[vmem] * 7,
        out_specs=(vmem,) * 4,
        scratch_shapes=[
            pltpu.VMEM((model, value), BF16),
            pltpu.VMEM((6 * rank, wide), BF16),
            pltpu.VMEM((2, 2 * rank, wide), BF16),
            pltpu.VMEM((2, 2 * rank, wide), BF16),
            pltpu.VMEM((2, 2 * rank, wide), BF16),
            pltpu.VMEM((2, 2 * rank, ranks), BF16),
            pltpu.VMEM((token_count, value), F32),
            dma((planes,)), dma((planes,)),
            dma(((planes + 1) * chips,)), dma(((planes + 1) * chips,)),
            dma((planes * chips,)), dma((planes * chips,)),
            dma((2 * planes * chips,)), dma((2 * planes * chips,)),
            dma((2,)), dma((2,)), dma((2,)), dma((2,)), dma((2,)), dma((2,)),
        ],
        compiler_params=pltpu.CompilerParams(
            collective_id=0, has_side_effects=True, vmem_limit_bytes=48 * 1024 * 1024
        ),
        cost_estimate=pl.CostEstimate(
            flops=4 * token_count * model * value,
            bytes_accessed=8 * token_count * model,
            transcendentals=0,
        ),
    )(
        tokens, output_cotangent, weight,
        lowering.reshape(ranks, model), raising.reshape(ranks, value), mask, sel,
    )
    return (
        proj, tgrad,
        gdown.reshape(stored, rank, model), gup.reshape(stored, rank, value),
    )


def solution(mesh):
    rows = P(("group", "dp"), None)
    stacks = P(("group", "dp"), None, None)
    return jax.shard_map(
        body,
        mesh=mesh,
        in_specs=(rows, rows, P("dp", None), stacks, stacks, P(("group", "dp")), P("group")),
        out_specs=(rows, rows, stacks, stacks),
        check_vma=False,
    )
```
